256 devices in a mesh: row: 64 (over x_hi, y, z), rep: 4 (over x_lo, core).
Axes of the slice: x: 4 (x_hi: 2, x_lo: 2; x = x_hi * 2 + x_lo), y: 4, z: 8, core: 2. Of those that a mesh axis runs over, the one named last changes fastest.
Arguments:
- features: bfloat16 [65536, 256], P(('row', 'rep')), may hold values from -1 to 2
- degree: int32 [65536], P(('row', 'rep')), may hold values from 1472 to 5889
- tiles: bfloat16 [64, 4, 16, 22, 128, 128], P('row', 'rep'), may hold values from 0 to 1, as said below
- tile_rows: int32 [64, 4, 16, 22], P('row', 'rep'), may hold values from 0 to 7, as said below
- tile_cols: int32 [64, 4, 16, 22], P('row', 'rep'), may hold values from 0 to 7
- live: int32 [64, 4, 16], P('row', 'rep'), may hold values from 1 to 22, as said below
- weight: bfloat16 [256, 256], replicated, may hold values from -0.375 to 0.375
Outputs:
- activated: bfloat16 [65536, 256], P(('row', 'rep'))
The draws below stay inside these ranges and needn't reach their ends.
Inputs may be any that keep to these rules, and one draw needn't show every extreme that they name: `tiles`: tile entries are 0 or 1. Within one list (one r, q, k) the pairs (tile_rows, tile_cols) of all 22 slots are distinct. `live`: in every draw all lists of one row shard use all 22 slots.
All inputs are finite; a program needn't handle non-finite values.
Results may differ from the reference program's by a relative error of at most 0.0031.
Values may be sent and summed in bfloat16 or wider, within the bound.
No kernel may reach another device: no remote copies, remote signals or barrier semaphores. Data moves between devices by JAX's collectives and lax.ppermute only.
A program may use at most 64 MiB of HBM per device.

```python
import jax
import jax.numpy as jnp
from jax import lax

F = 256
TILE = 128
RB = 8
SLOTS = 22
ROWS = 1024
NODES = 65536
STEPS = 16
N_ROW = 64
N_REP = 4


def pair_table(key):
    scores = jax.random.randint(key, (N_ROW, N_REP, STEPS, RB * RB), 0, 1 << 20)
    order = jnp.argsort(scores * (RB * RB) + jnp.arange(RB * RB, dtype=jnp.int32), axis=-1)
    return order[..., :SLOTS].astype(jnp.int32)


def draw_tiles(key, part):
    key = jax.random.fold_in(key, 11)
    values = jax.random.bernoulli(key, 0.25, (N_ROW, N_REP, STEPS, SLOTS, TILE, TILE)).astype(jnp.float32)
    return values.astype(jnp.bfloat16)


def draw_tile_rows(key, part):
    pairs = pair_table(jax.random.fold_in(key, 7))
    return pairs // RB


def draw_tile_cols(key, part):
    pairs = pair_table(jax.random.fold_in(key, 7))
    return pairs % RB


def draw_live(key, part):
    key = jax.random.fold_in(key, 13)
    first, second = jax.random.split(key)
    counts = jax.random.randint(first, (N_ROW, N_REP, STEPS), 1, SLOTS + 1)
    heavy = jax.random.randint(second, (), 0, N_ROW)
    shard_ids = jnp.arange(N_ROW, dtype=jnp.int32)[:, None, None]
    return jnp.where(shard_ids == heavy, SLOTS, counts).astype(jnp.int32)


def with_ends(values, rng, low, top_value):
    shape = values.shape
    index_at = [jax.random.randint(jax.random.fold_in(rng, axis), (), 0, shape[axis]) for axis in range(len(shape))]
    values = values.at[tuple(index_at)].set(low)
    longest = shape.index(max(shape))
    index_at[longest] = (index_at[longest] + 1) % shape[longest]
    return values.at[tuple(index_at)].set(top_value)


def levels(own_key, shape, shards, low, high):
    loudness = 1.0
    for dim, blocks in shards:
        steps = jax.random.uniform(jax.random.fold_in(jax.random.fold_in(own_key, 6), dim), (blocks,), jnp.float32, low / len(shards), high / len(shards))
        loudness = loudness * jnp.repeat(jnp.exp(steps), shape[dim] // blocks).reshape((-1,) + (1,) * (len(shape) - 1 - dim))
    return loudness


def centred(rng, dims, deviation, reach, held_as=jnp.bfloat16):
    values = jax.random.normal(rng, dims, jnp.float32) * deviation
    return jnp.minimum(jnp.maximum(values, -reach), reach).astype(held_as)


def setup_inputs(seed: int = 0) -> dict:
    key_list = jax.random.split(jax.random.key(seed), 8)
    features = jnp.clip(-1.0 + 3.0 * jax.random.uniform(key_list[0], (NODES, F), jnp.float32) ** levels(key_list[0], (NODES, F), ((0, 256),), -0.2, 0.2), -1.0, 2.0).astype(jnp.bfloat16)
    degree = with_ends(jax.random.randint(key_list[1], (NODES,), max(1, (SLOTS + 1) * TILE * N_ROW // (16 * RB)), (SLOTS + 1) * TILE * N_ROW // (4 * RB) + 2), jax.random.fold_in(key_list[1], 1), max(1, (SLOTS + 1) * TILE * N_ROW // (16 * RB)), ((SLOTS + 1) * TILE * N_ROW // (4 * RB) + 2) - 1).astype(jnp.int32)
    tiles = draw_tiles(jax.random.fold_in(key_list[7], 71), 0)
    tile_rows = draw_tile_rows(jax.random.fold_in(key_list[7], 71), 0)
    tile_cols = draw_tile_cols(jax.random.fold_in(key_list[7], 71), 0)
    live = draw_live(jax.random.fold_in(key_list[7], 71), 0)
    weight = centred(key_list[6], (F, F), F ** -0.5, 0.375)
    return dict(features=features, degree=degree, tiles=tiles, tile_rows=tile_rows, tile_cols=tile_cols, live=live, weight=weight)


def reference(features, degree, tiles, tile_rows, tile_cols, live, weight):
    scale = lax.rsqrt(degree.astype(jnp.float32))
    scaled = (features.astype(jnp.float32) * scale[:, None]).astype(jnp.bfloat16)
    blocks = scaled.reshape(N_ROW, RB, TILE, F)
    step_ids = jnp.arange(STEPS, dtype=jnp.int32)
    rep_ids = jnp.arange(N_REP, dtype=jnp.int32)
    slot_ids = jnp.arange(SLOTS, dtype=jnp.int32)
    block_ids = jnp.arange(RB, dtype=jnp.int32)

    def one_shard(shard):
        source = (shard - rep_ids[:, None] - N_REP * step_ids[None, :]) % N_ROW
        mine = lax.dynamic_index_in_dim(tiles, shard, 0, keepdims=False)
        dest = lax.dynamic_index_in_dim(tile_rows, shard, 0, keepdims=False)
        cols = lax.dynamic_index_in_dim(tile_cols, shard, 0, keepdims=False)
        counts = lax.dynamic_index_in_dim(live, shard, 0, keepdims=False)
        picked = blocks[source[:, :, None], cols]
        products = jnp.einsum('qksij,qksjf->qksif', mine.astype(jnp.float32), picked.astype(jnp.float32), precision=lax.Precision.HIGHEST)
        alive = slot_ids[None, None, :] < counts[:, :, None]
        onehot = ((dest[..., None] == block_ids) & alive[..., None]).astype(jnp.float32)
        summed = jnp.einsum('qksb,qksif->bif', onehot, products, precision=lax.Precision.HIGHEST)
        return summed.reshape(ROWS, F)
    gathered = lax.map(one_shard, jnp.arange(N_ROW, dtype=jnp.int32)).reshape(NODES, F)
    normed = gathered * scale[:, None]
    product = jnp.dot(normed, weight.astype(jnp.float32), precision=lax.Precision.HIGHEST)
    return jax.nn.relu(product).astype(jnp.bfloat16)
```

```python
import functools

import jax
import jax.numpy as jnp
import numpy as np
from jax import lax
from jax.experimental import pallas as pl
from jax.experimental.pallas import tpu as pltpu
from jax.sharding import PartitionSpec as P

AXES = ("row", "rep")
TILE = 128
SLOTS = 22
STEPS = 16
N_TILES = STEPS * SLOTS
LIST = 256


def home_shift(q):
    return (0, 1, 2, -1)[q]


def route(dh=0, dp=0, dy=0, home=False):
    out = []
    for h in range(2):
        for y in range(4):
            for z in range(8):
                for q in range(4):
                    hh, zz, qq = h, z, q
                    for _ in range(dp):
                        hh, zz, qq = hh + (qq == 3), zz + 1, (qq + 1) % 4
                    for _ in range(-dp):
                        hh, zz, qq = hh - (qq == 0), zz - 1, (qq - 1) % 4
                    if home:
                        zz -= home_shift(qq)
                    source = ((((hh + dh) % 2) * 4 + (y + dy) % 4) * 8 + zz % 8) * 4 + qq
                    out.append((source, ((h * 4 + y) * 8 + z) * 4 + q))
    return out


class Blocks:
    def __init__(self, rows, labels):
        self.rows, self.labels = rows, labels

    def __getitem__(self, blocks):
        first, last = blocks.start or 0, len(self.labels) if blocks.stop is None else blocks.stop
        return Blocks(lax.slice_in_dim(self.rows, first * TILE, last * TILE), self.labels[first:last])

    def moved(self, dh=0, dp=0, dy=0, home=False):
        rows = lax.ppermute(self.rows, AXES, route(dh, dp, dy, home))
        labels = [(t, (a + dh) % 2, (b + dp) % 8, (c + dy) % 4) for t, a, b, c in self.labels]
        return Blocks(rows, labels)


def joined(*parts):
    return Blocks(jnp.concatenate([p.rows for p in parts], 0), [label for p in parts for label in p.labels])


def gather(scaled):
    own = Blocks(scaled, [(0, 0, 0, 0), (1, 0, 0, 0)])
    near, far = own.moved(home=True), own.moved(dh=1, home=True)
    start = joined(near[0:1], far[0:1], near[1:2], far[1:2])
    found = [start]

    def along_y(blocks):
        got = [blocks.moved(dy=dy) for dy in (1, -1, 2)]
        found.extend(got)
        return got

    along = along_y(start)
    up, down = start.moved(dp=1), start.moved(dp=-1)
    found.extend((up, down))
    others = joined(*(a[2:4] for a in along))
    along_y(joined(up[0:2], down[0:2]))
    up, down = joined(up, others).moved(dp=1), joined(down, others).moved(dp=-1)
    found.extend((up, down))
    along_y(joined(up[0:2], down[0:2]))
    up, down = up.moved(dp=1), down.moved(dp=-1)
    found.extend((up, down))
    along_y(joined(up[0:2], down[0:2]))
    up, down = joined(up[0:1], up[2:3], up[4:10]).moved(dp=1), joined(down[1:2], down[3:4], down[4:10]).moved(dp=-1)
    found.extend((up, down))
    along_y(joined(up[0:1], down[0:1]))
    found.extend((up[2:5].moved(dp=1), down[5:8].moved(dp=-1)))
    return found


def list_kernel(live, coded, places, lists, counts):
    for b in range(8):
        counts[b] = 0

    def one_source(k, _):
        def one_slot(s, _):
            v = coded[k, s]
            b = v >> 7
            n = counts[b]
            lists[b, n] = (k * SLOTS + s) + (places[v & 127] << 10)
            counts[b] = n + 1
            return 0

        return lax.fori_loop(0, live[k], one_slot, 0)

    lax.fori_loop(0, STEPS, one_source, 0)
    for b in range(8):
        lists[b, counts[b]] = N_TILES


def slot_lists(live, coded, places):
    smem = pl.BlockSpec(memory_space=pltpu.SMEM)
    return pl.pallas_call(
        list_kernel,
        out_shape=(jax.ShapeDtypeStruct((8, LIST), jnp.int32), jax.ShapeDtypeStruct((8,), jnp.int32)),
        in_specs=[smem] * 3,
        out_specs=(smem, smem),
        cost_estimate=pl.CostEstimate(flops=0, bytes_accessed=20000, transcendentals=0),
    )(live, coded, places)


def product_kernel(sizes, place, lists, counts, tiles, *refs):
    sources, (keep, send, held, blocks, tile_sems, block_sems) = refs[: len(sizes)], refs[len(sizes) :]
    copies = [
        pltpu.make_async_copy(tiles.at[pl.ds(k * SLOTS, SLOTS)], held.at[pl.ds(k * SLOTS, SLOTS)], tile_sems.at[k])
        for k in range(STEPS)
    ]
    first = 0
    for i, size in enumerate(sizes):
        copies.append(pltpu.make_async_copy(sources[i], blocks.at[pl.ds(first, size)], block_sems.at[i]))
        first += size
    for copy in copies:
        copy.start()
    held[N_TILES] = jnp.zeros((TILE, TILE), jnp.bfloat16)
    for copy in copies:
        copy.wait()
    mine = place[0]
    for b in range(8):

        def pair(i, total):
            one, two = lists[b, 2 * i], lists[b, 2 * i + 1]
            left = jnp.concatenate([held[one & 1023], held[two & 1023]], axis=1)
            right = jnp.concatenate([blocks[one >> 10], blocks[two >> 10]], axis=0)
            return total + jnp.dot(left, right, preferred_element_type=jnp.float32)

        total = lax.fori_loop(0, (counts[b] + 1) >> 1, pair, jnp.zeros((TILE, 256), jnp.float32))
        other = (b >> 1) ^ mine
        rows = pl.ds((b & 1) * TILE, TILE)

        @pl.when((other & 1) == 0)
        def _():
            keep[other >> 1, rows, :] = total

        @pl.when((other & 1) == 1)
        def _():
            send[other >> 1, rows, :] = total


def products(place, lists, counts, tiles, found):
    smem, anywhere = pl.BlockSpec(memory_space=pltpu.SMEM), pl.BlockSpec(memory_space=pl.ANY)
    vmem = pl.BlockSpec(memory_space=pltpu.VMEM)
    sizes = tuple(len(f.labels) for f in found)
    half = jax.ShapeDtypeStruct((2, 256, 256), jnp.float32)
    return pl.pallas_call(
        functools.partial(product_kernel, sizes),
        out_shape=(half, half),
        in_specs=[smem] * 3 + [anywhere] * (1 + len(found)),
        out_specs=(vmem, vmem),
        scratch_shapes=[
            pltpu.VMEM((N_TILES + 1, TILE, TILE), jnp.bfloat16),
            pltpu.VMEM((sum(sizes), TILE, 256), jnp.bfloat16),
            pltpu.SemaphoreType.DMA((STEPS,)),
            pltpu.SemaphoreType.DMA((len(sizes),)),
        ],
        compiler_params=pltpu.CompilerParams(vmem_limit_bytes=40 << 20),
        cost_estimate=pl.CostEstimate(flops=3_000_000_000, bytes_accessed=20_000_000, transcendentals=0),
    )(place, lists, counts, tiles, *(f.rows.reshape(-1, TILE, 256) for f in found))


def local(features, degree, tiles, tile_rows, tile_cols, live, weight):
    row, mine = lax.axis_index("row"), lax.axis_index("rep")
    scale = lax.rsqrt(degree.astype(jnp.float32))
    scaled = (features.astype(jnp.float32) * scale[:, None]).astype(jnp.bfloat16)
    found = gather(scaled)

    cols, steps = tile_cols[0, 0], jnp.arange(STEPS, dtype=jnp.int32)[:, None]
    source = (row - mine - 4 * steps) & 63
    piece = cols >> 1
    shift = jnp.where(piece == 3, -1, piece)
    dp = ((source & 7) + shift - row) & 7
    dy = ((source >> 3) - (row >> 3)) & 3
    dh = ((source >> 5) - (row >> 5) - ((mine + dp) >> 2)) & 1
    coded = (((tile_rows[0, 0] * 2 + (cols & 1)) * 2 + dh) * 8 + dp) * 4 + dy
    places = np.zeros(128, np.int32)
    for n, (t, a, b, c) in enumerate(label for f in found for label in f.labels):
        places[((t * 2 + a) * 8 + b) * 4 + c] = n
    lists, counts = slot_lists(live[0, 0], coded, jnp.asarray(places))

    keep, send = products(mine[None], lists, counts, tiles.reshape(N_TILES, TILE, TILE), found)
    devices = range(256)
    halves = keep + lax.ppermute(send, AXES, [(i, i ^ 1) for i in devices])
    share = halves[0] + lax.ppermute(halves[1], AXES, [(i, i ^ 2) for i in devices])
    normed = share * scale[:, None]
    product = jnp.dot(normed, weight.astype(jnp.float32), precision=lax.Precision.HIGHEST)
    return jax.nn.relu(product).astype(jnp.bfloat16)


def solution(mesh):
    in_specs = (
        P(("row", "rep"), None),
        P(("row", "rep")),
        P("row", "rep", None, None, None, None),
        P("row", "rep", None, None),
        P("row", "rep", None, None),
        P("row", "rep", None),
        P(),
    )
    out_specs = P(("row", "rep"), None)
    return jax.shard_map(local, mesh=mesh, in_specs=in_specs, out_specs=out_specs, check_vma=False)
```

```python
import functools

import jax
import jax.numpy as jnp
import numpy as np
from jax import lax
from jax.experimental import pallas as pl
from jax.experimental.pallas import tpu as pltpu
from jax.sharding import PartitionSpec as P

AXES = ("row", "rep")
TILE = 128
SLOTS = 22
STEPS = 16
N_TILES = STEPS * SLOTS
LIST = 128
BATCH = 4
PHASES = 5

HOME = (0, 1, 2, -1)


def member(h, y, z, q):
    return (((h % 2) * 4 + y % 4) * 8 + z % 8) * 4 + q % 4


def up(h, y, z, q):
    return member(h + (q == 3), y, z + 1, q + 1)


def down(h, y, z, q):
    return member(h - (q == 0), y, z - 1, q - 1)


MOVES = {
    "home": (lambda h, y, z, q: member(h, y, z - HOME[q], q), lambda t, h, p, e: (t, h, p, e)),
    "far": (lambda h, y, z, q: member(h + 1, y, z - HOME[q], q), lambda t, h, p, e: (t, 1 - h, p, e)),
    "z1": (lambda *d: down(*d) if d[3] % 2 else up(*d), lambda t, h, p, e: (t, h, (1 - p) % 8, e)),
    "z2": (lambda *d: up(*d) if d[3] % 2 else down(*d), lambda t, h, p, e: (t, h, (-1 - p) % 8, e)),
    "y1": (lambda h, y, z, q: member(h, y ^ (3 if q % 2 else 1), z, q), lambda t, h, p, e: (t, h, p, e ^ 1)),
    "y2": (lambda h, y, z, q: member(h, y ^ (1 if q % 2 else 3), z, q), lambda t, h, p, e: (t, h, p, e ^ 2)),
}


class Blocks:
    def __init__(self, rows, labels):
        self.rows, self.labels = rows, labels

    def __getitem__(self, blocks):
        first, last = blocks.start or 0, len(self.labels) if blocks.stop is None else blocks.stop
        return Blocks(lax.slice_in_dim(self.rows, first * TILE, last * TILE), self.labels[first:last])

    def moved(self, kind):
        sender, relabel = MOVES[kind]
        here = [(h, y, z, q) for h in range(2) for y in range(4) for z in range(8) for q in range(4)]
        rows = lax.ppermute(self.rows, AXES, [(sender(*d), member(*d)) for d in here])
        return Blocks(rows, [relabel(*label) for label in self.labels])

    def half(self, t):
        runs, first = [], 0
        for last in range(1, len(self.labels) + 1):
            if last == len(self.labels) or self.labels[last][0] != self.labels[first][0]:
                if self.labels[first][0] == t:
                    runs.append(self[first:last])
                first = last
        return joined(*runs)


def joined(*parts):
    return Blocks(jnp.concatenate([p.rows for p in parts], 0), [label for p in parts for label in p.labels])


def in_order(parts, *earlier):
    rows = lax.optimization_barrier(tuple(p.rows for p in parts) + earlier)
    return [Blocks(r, p.labels) for r, p in zip(rows, parts)]


def gather(scaled, first_ready, ready, add):
    own = Blocks(scaled, [(0, 0, 0, 0), (1, 0, 0, 0)])
    near, far = own.moved("home"), own.moved("far")
    (s0,) = in_order([joined(near[0:1], far[0:1], near[1:2], far[1:2])], first_ready)
    s1, e1 = s0.moved("z1"), s0.moved("y1")
    s2, e2 = joined(s0, s1).moved("z2"), joined(s0, e1).moved("y2")
    b0 = joined(e1.half(1), e2.half(1))
    z, y1 = in_order([joined(s2, b0), joined(s1.half(0), s2.half(0))], ready)
    z3, y1a = z.moved("z1"), y1.moved("y1")
    total = add(None, [s0, s1, e1, s2, e2])
    z, y = in_order([joined(z3[0:8], b0, z3[8:14]), joined(y1, y1a)], total)
    z4, y1b = z.moved("z2"), y.moved("y2")
    total = add(total, [z3, y1a])
    b, y2 = in_order([z4[8:20], joined(z3[0:8].half(0), z4[0:8].half(0))], total)
    b3, y2a = b.moved("z1"), y2.moved("y1")
    total = add(total, [z4, y1b])
    b, y = in_order([b3, joined(y2, y2a)], total)
    b4, y2b = b.moved("z2"), y.moved("y2")
    total = add(total, [b3, y2a])
    return add(total, [b4, y2b])


def phase_labels():
    found = []

    def traced(rows):
        return gather(rows, rows, rows, lambda _, parts: found.append([label for p in parts for label in p.labels]) or rows)

    jax.eval_shape(traced, jax.ShapeDtypeStruct((2 * TILE, 256), jnp.bfloat16))
    return found


def list_kernel(live, coded, tiles, lists, counts, held, sem):
    load = pltpu.make_async_copy(tiles, held, sem)
    load.start()
    for b in range(8 * PHASES):
        counts[b] = 0

    def one_source(k, _):
        def one_slot(s, _):
            v = coded[k, s]
            b = v >> 17
            n = counts[b]
            lists[b, n] = v & 0x1FFFF
            counts[b] = n + 1
            return 0

        return lax.fori_loop(0, live[k], one_slot, 0)

    lax.fori_loop(0, STEPS, one_source, 0)
    for b in range(8 * PHASES):
        for i in range(BATCH - 1):
            lists[b, counts[b] + i] = 0
    load.wait()


def slot_lists(live, coded, tiles):
    smem, vmem = pl.BlockSpec(memory_space=pltpu.SMEM), pl.BlockSpec(memory_space=pltpu.VMEM)
    return pl.pallas_call(
        list_kernel,
        out_shape=(
            jax.ShapeDtypeStruct((8 * PHASES, LIST), jnp.int32),
            jax.ShapeDtypeStruct((8 * PHASES,), jnp.int32),
            jax.ShapeDtypeStruct(tiles.shape, tiles.dtype),
        ),
        in_specs=[smem, smem, pl.BlockSpec(memory_space=pltpu.HBM)],
        out_specs=(smem, smem, vmem),
        scratch_shapes=[pltpu.SemaphoreType.DMA],
        compiler_params=pltpu.CompilerParams(vmem_limit_bytes=42 << 20),
        cost_estimate=pl.CostEstimate(flops=0, bytes_accessed=23_000_000, transcendentals=0),
    )(live, coded, tiles)


def product_kernel(buckets, first_bucket, more, lists, counts, tiles, blocks, *refs):
    before, total = refs if more else (None, refs[0])
    for b in range(buckets):

        def batch(i, total, b=b):
            at = [lists[first_bucket + b, i * BATCH + j] for j in range(BATCH)]
            left = jnp.concatenate([tiles[a & 1023] for a in at], axis=1)
            right = jnp.concatenate([blocks[a >> 10] for a in at], axis=0)
            return total + jnp.dot(left, right, preferred_element_type=jnp.float32)

        rows = pl.ds((b % 2) * TILE, TILE)
        start = before[b // 2, rows, :] if more else jnp.zeros((TILE, 256), jnp.float32)
        n = (counts[first_bucket + b] + (BATCH - 1)) // BATCH
        total[b // 2, rows, :] = lax.fori_loop(0, n, batch, start)


def products(lists, counts, first_bucket, buckets, tiles, blocks, before=None):
    smem, vmem = pl.BlockSpec(memory_space=pltpu.SMEM), pl.BlockSpec(memory_space=pltpu.VMEM)
    more = before is not None
    slots = blocks.shape[0] * 3 * buckets // 8
    return pl.pallas_call(
        functools.partial(product_kernel, buckets, first_bucket, more),
        out_shape=jax.ShapeDtypeStruct((buckets // 2, 256, 256), jnp.float32),
        in_specs=[smem] * 2 + [vmem] * (2 + more),
        out_specs=vmem,
        compiler_params=pltpu.CompilerParams(vmem_limit_bytes=2 << 20),
        cost_estimate=pl.CostEstimate(flops=slots * 8_400_000, bytes_accessed=slots * 150_000, transcendentals=0),
    )(lists, counts, tiles, blocks, *([before] if more else []))


def local(features, degree, tiles, tile_rows, tile_cols, live, weight):
    row, mine = lax.axis_index("row"), lax.axis_index("rep")
    scale = lax.rsqrt(degree.astype(jnp.float32))
    scaled = (features.astype(jnp.float32) * scale[:, None]).astype(jnp.bfloat16)

    cols, steps = tile_cols[0, 0], jnp.arange(STEPS, dtype=jnp.int32)[:, None]
    source = (row - mine - 4 * steps) & 63
    piece, t = cols >> 1, cols & 1
    p = ((source & 7) + jnp.where(piece == 3, -1, piece) - row) & 7
    h = ((source >> 5) - (row >> 5) - ((mine + p) >> 2)) & 1
    core = mine & 1
    p = jnp.where(core == 1, -p & 7, p)
    y = ((source >> 3) ^ (row >> 3)) & 3
    swapped = jnp.where(t == 0, core, piece & 1)
    e = jnp.where(y == 2, 3, jnp.where(y == 0, 0, jnp.where(y == 1, 1 + swapped, 2 - swapped)))
    dest = tile_rows[0, 0]
    bucket = ((((dest >> 1) ^ mine) ^ 2) << 1) + (dest & 1)
    label = (((t * 2 + h) * 8 + p) * 4 + e)[..., None]
    places = np.zeros(128, np.int32)
    for n, found in enumerate(phase_labels()):
        for i, (t, h, p, e) in enumerate(found):
            places[((t * 2 + h) * 8 + p) * 4 + e] = ((8 * n) << 17) + ((i + 1) << 10)
    place = jnp.sum(jnp.where(label == jnp.arange(128, dtype=jnp.int32), jnp.asarray(places), 0), axis=-1)
    coded = place + (bucket << 17) + steps * SLOTS + jnp.arange(SLOTS, dtype=jnp.int32)
    lists, counts, held = slot_lists(live[0, 0], coded, tiles.reshape(N_TILES, TILE, TILE))
    devices = range(256)
    nothing = jnp.zeros((TILE, 256), jnp.bfloat16)
    n = 0

    def add(total, found):
        nonlocal n
        first, n = 8 * n, n + 1
        blocks = jnp.concatenate([nothing] + [f.rows for f in found], 0).reshape(-1, TILE, 256)
        if n < PHASES:
            return products(lists, counts, first, 8, held, blocks, total)
        theirs = to_owner_core(products(lists, counts, first, 4, held, blocks, total[0:2]))
        theirs, total = lax.optimization_barrier((theirs, total))
        theirs = lax.ppermute(theirs, AXES, [(i, i ^ 2) for i in devices])
        return to_owner_core(products(lists, counts, first + 4, 4, held, blocks, total[2:4])), theirs

    def to_owner_core(part):
        return part[0] + lax.ppermute(part[1], AXES, [(i, i ^ 1) for i in devices])

    def weighted(share):
        return jnp.dot(share * scale[:, None], weight.astype(jnp.float32), precision=lax.Precision.HIGHEST)

    ours, theirs = gather(scaled, coded, counts, add)
    return jax.nn.relu(weighted(ours) + weighted(theirs)).astype(jnp.bfloat16)


def solution(mesh):
    in_specs = (
        P(("row", "rep"), None),
        P(("row", "rep")),
        P("row", "rep", None, None, None, None),
        P("row", "rep", None, None),
        P("row", "rep", None, None),
        P("row", "rep", None),
        P(),
    )
    out_specs = P(("row", "rep"), None)
    return jax.shard_map(local, mesh=mesh, in_specs=in_specs, out_specs=out_specs, check_vma=False)
```

```python
import functools

import jax
import jax.numpy as jnp
import numpy as np
from jax import lax
from jax.experimental import pallas as pl
from jax.experimental.pallas import tpu as pltpu
from jax.sharding import PartitionSpec as P

AXES = ("row", "rep")
TILE = 128
SLOTS = 22
STEPS = 16
N_TILES = STEPS * SLOTS
LIST = 128
BATCH = 4
AT_ONCE = 3
PHASES = 5

HOME = (0, 1, 2, -1)


def member(h, y, z, q):
    return (((h % 2) * 4 + y % 4) * 8 + z % 8) * 4 + q % 4


def up(h, y, z, q):
    return member(h + (q == 3), y, z + 1, q + 1)


def down(h, y, z, q):
    return member(h - (q == 0), y, z - 1, q - 1)


MOVES = {
    "home": (lambda h, y, z, q: member(h, y, z - HOME[q], q), lambda t, h, p, e: (t, h, p, e)),
    "far": (lambda h, y, z, q: member(h + 1, y, z - HOME[q], q), lambda t, h, p, e: (t, 1 - h, p, e)),
    "z1": (lambda *d: down(*d) if d[3] % 2 else up(*d), lambda t, h, p, e: (t, h, (1 - p) % 8, e)),
    "z2": (lambda *d: up(*d) if d[3] % 2 else down(*d), lambda t, h, p, e: (t, h, (-1 - p) % 8, e)),
    "y1": (lambda h, y, z, q: member(h, y ^ (3 if q % 2 else 1), z, q), lambda t, h, p, e: (t, h, p, e ^ 1)),
    "y2": (lambda h, y, z, q: member(h, y ^ (1 if q % 2 else 3), z, q), lambda t, h, p, e: (t, h, p, e ^ 2)),
}


class Blocks:
    def __init__(self, rows, labels):
        self.rows, self.labels = rows, labels

    def __getitem__(self, blocks):
        first, last = blocks.start or 0, len(self.labels) if blocks.stop is None else blocks.stop
        return Blocks(lax.slice_in_dim(self.rows, first * TILE, last * TILE), self.labels[first:last])

    def moved(self, kind):
        sender, relabel = MOVES[kind]
        here = [(h, y, z, q) for h in range(2) for y in range(4) for z in range(8) for q in range(4)]
        rows = lax.ppermute(self.rows, AXES, [(sender(*d), member(*d)) for d in here])
        return Blocks(rows, [relabel(*label) for label in self.labels])

    def half(self, t):
        runs, first = [], 0
        for last in range(1, len(self.labels) + 1):
            if last == len(self.labels) or self.labels[last][0] != self.labels[first][0]:
                if self.labels[first][0] == t:
                    runs.append(self[first:last])
                first = last
        return joined(*runs)


def joined(*parts):
    return Blocks(jnp.concatenate([p.rows for p in parts], 0), [label for p in parts for label in p.labels])


def in_order(parts, *earlier):
    rows = lax.optimization_barrier(tuple(p.rows for p in parts) + earlier)
    return [Blocks(r, p.labels) for r, p in zip(rows, parts)]


def gather(scaled, first_ready, prepare, add):
    own = Blocks(scaled, [(0, 0, 0, 0), (1, 0, 0, 0)])
    near, far = own.moved("home"), own.moved("far")
    (s0,) = in_order([joined(near[0:1], far[0:1], near[1:2], far[1:2])], first_ready)
    s1, e1 = in_order([s0.moved("z1"), s0.moved("y1")])
    ready = prepare(s1.rows)
    s2, e2 = in_order([joined(s0, s1).moved("z2"), joined(s0, e1).moved("y2")], ready)
    b0 = joined(e1.half(1), e2.half(1))
    y12 = joined(s1.half(0), s2.half(0))
    z3, y3 = joined(s2, b0).moved("z1"), y12.moved("y1")
    total = add(None, [s0, s1, e1, s2, e2])
    s3 = z3[0:8].half(0)
    z, y = in_order([joined(z3[0:8], b0, z3[8:14]), joined(y12, y3, s3)], total)
    z4, y4 = z.moved("z2"), y.moved("y2")
    total = add(total, [z3, y3])
    s4 = z4[0:8].half(0)
    z, y = in_order([z4[8:20], joined(s3, y4[12:16], s4)], total)
    z5, y5 = z.moved("z1"), y.moved("y1")
    total = add(total, [z4])
    z, y = in_order([z5, joined(s4, y5[8:12])], total)
    z6, y6 = z.moved("z2"), y.moved("y2")
    total = add(total, [y4, z5, y5])
    return add(total, [z6, y6])


def phase_labels():
    found = []

    def traced(rows):
        return gather(rows, rows, lambda _: rows, lambda _, parts: found.append([label for p in parts for label in p.labels]) or rows)

    jax.eval_shape(traced, jax.ShapeDtypeStruct((2 * TILE, 256), jnp.bfloat16))
    return found


def list_kernel(live, coded, tiles, lists, counts, held, sem):
    load = pltpu.make_async_copy(tiles, held, sem)
    load.start()
    for b in range(8 * PHASES):
        counts[b] = 0

    def one_source(k, _):
        used = live[k]
        for s in range(SLOTS):

            @pl.when(s < used)
            def _(s=s):
                v = coded[k, s]
                b = v >> 17
                n = counts[b]
                lists[b, n] = v & 0x1FFFF
                counts[b] = n + 1

        return 0

    lax.fori_loop(0, STEPS, one_source, 0)
    for b in range(8 * PHASES):
        for i in range(BATCH - 1):
            lists[b, counts[b] + i] = 0
    for i in range(BATCH):
        lists[8 * PHASES, i] = 0
    load.wait()


def slot_lists(live, coded, tiles):
    smem, vmem = pl.BlockSpec(memory_space=pltpu.SMEM), pl.BlockSpec(memory_space=pltpu.VMEM)
    return pl.pallas_call(
        list_kernel,
        out_shape=(
            jax.ShapeDtypeStruct((8 * PHASES + 1, LIST), jnp.int32),
            jax.ShapeDtypeStruct((8 * PHASES,), jnp.int32),
            jax.ShapeDtypeStruct(tiles.shape, tiles.dtype),
        ),
        in_specs=[smem, smem, pl.BlockSpec(memory_space=pltpu.HBM)],
        out_specs=(smem, smem, vmem),
        scratch_shapes=[pltpu.SemaphoreType.DMA],
        compiler_params=pltpu.CompilerParams(vmem_limit_bytes=42 << 20),
        cost_estimate=pl.CostEstimate(flops=0, bytes_accessed=23_000_000, transcendentals=0),
    )(live, coded, tiles)


def product_kernel(buckets, first_bucket, more, lists, counts, tiles, blocks, *refs):
    before, total, order = refs if more else (None, *refs)
    total[...] = before[...] if more else jnp.zeros_like(total)
    end = 0
    for b in range(buckets):

        def note(i, end, b=b):
            order[end] = (b << 16) + ((first_bucket + b) << 8) + i
            return end + 1

        end = lax.fori_loop(0, (counts[first_bucket + b] + (BATCH - 1)) // BATCH, note, end)
    for i in range(AT_ONCE - 1):
        order[end + i] = (8 * PHASES) << 8

    def batches(g, _):
        found = []
        for i in range(AT_ONCE):
            v = order[g * AT_ONCE + i]
            at = [lists[(v >> 8) & 255, (v & 255) * BATCH + j] for j in range(BATCH)]
            left = jnp.concatenate([tiles[a & 1023] for a in at], axis=1)
            right = jnp.concatenate([blocks[a >> 10] for a in at], axis=0)
            found.append((v >> 16, jnp.dot(left, right, preferred_element_type=jnp.float32)))
        for b, product in found:
            total[b >> 1, pl.ds((b & 1) * TILE, TILE), :] += product
        return 0

    lax.fori_loop(0, (end + (AT_ONCE - 1)) // AT_ONCE, batches, 0)


def products(lists, counts, first_bucket, buckets, tiles, blocks, before=None):
    smem, vmem = pl.BlockSpec(memory_space=pltpu.SMEM), pl.BlockSpec(memory_space=pltpu.VMEM)
    more = before is not None
    slots = blocks.shape[0] * 3 * buckets // (8 if buckets < 8 else 32)
    return pl.pallas_call(
        functools.partial(product_kernel, buckets, first_bucket, more),
        out_shape=jax.ShapeDtypeStruct((buckets // 2, 256, 256), jnp.float32),
        in_specs=[smem] * 2 + [vmem] * (2 + more),
        out_specs=vmem,
        scratch_shapes=[pltpu.SMEM((N_TILES // BATCH + 8 + AT_ONCE,), jnp.int32)],
        compiler_params=pltpu.CompilerParams(vmem_limit_bytes=2 << 20),
        cost_estimate=pl.CostEstimate(flops=slots * 8_400_000, bytes_accessed=slots * 150_000, transcendentals=0),
    )(lists, counts, tiles, blocks, *([before] if more else []))


def local(features, degree, tiles, tile_rows, tile_cols, live, weight):
    row, mine = lax.axis_index("row"), lax.axis_index("rep")
    scale = lax.rsqrt(lax.optimization_barrier(degree).astype(jnp.float32))
    first_scale = lax.rsqrt(degree.astype(jnp.float32))
    scaled = (features.astype(jnp.float32) * first_scale[:, None]).astype(jnp.bfloat16)

    cols, steps = tile_cols[0, 0], jnp.arange(STEPS, dtype=jnp.int32)[:, None]
    source = (row - mine - 4 * steps) & 63
    piece, t = cols >> 1, cols & 1
    p = ((source & 7) + jnp.where(piece == 3, -1, piece) - row) & 7
    h = ((source >> 5) - (row >> 5) - ((mine + p) >> 2)) & 1
    core = mine & 1
    p = jnp.where(core == 1, -p & 7, p)
    y = ((source >> 3) ^ (row >> 3)) & 3
    swapped = jnp.where(t == 0, core, piece & 1)
    e = jnp.where(y == 2, 3, jnp.where(y == 0, 0, jnp.where(y == 1, 1 + swapped, 2 - swapped)))
    dest = tile_rows[0, 0]
    bucket = ((((dest >> 1) ^ mine) ^ 2) << 1) + (dest & 1)
    label = (((t * 2 + h) * 8 + p) * 4 + e)[..., None]
    places = np.zeros(128, np.int32)
    for n, found in enumerate(phase_labels()):
        for i, (t, h, p, e) in enumerate(found):
            places[((t * 2 + h) * 8 + p) * 4 + e] = ((8 * n) << 17) + ((i + 1) << 10)
    place = jnp.sum(jnp.where(label == jnp.arange(128, dtype=jnp.int32), jnp.asarray(places), 0), axis=-1)
    coded = place + (bucket << 17) + steps * SLOTS + jnp.arange(SLOTS, dtype=jnp.int32)
    lists, counts, held = None, None, None
    devices = range(256)
    nothing = jnp.zeros((TILE, 256), jnp.bfloat16)
    n = 0

    def prepare(earlier):
        nonlocal lists, counts, held
        now, _ = lax.optimization_barrier((coded, earlier))
        lists, counts, held = slot_lists(live[0, 0], now, tiles.reshape(N_TILES, TILE, TILE))
        return counts

    def add(total, found):
        nonlocal n
        first, n = 8 * n, n + 1
        blocks = jnp.concatenate([nothing] + [f.rows for f in found], 0).reshape(-1, TILE, 256)
        if n < PHASES:
            return products(lists, counts, first, 8, held, blocks, total)
        theirs = to_owner_core(products(lists, counts, first, 4, held, blocks, total[0:2]))
        theirs, total = lax.optimization_barrier((theirs, total))
        theirs = lax.ppermute(theirs, AXES, [(i, i ^ 2) for i in devices])
        return to_owner_core(products(lists, counts, first + 4, 4, held, blocks, total[2:4]), 2), theirs

    def to_owner_core(part, pieces=1):
        size = part.shape[1] // pieces
        sent = [part[1, i * size : (i + 1) * size] for i in range(pieces)]
        got = [lax.ppermute(x, AXES, [(i, i ^ 1) for i in devices]) for x in sent]
        return part[0] + jnp.concatenate(got, 0)

    def weighted(share):
        return jnp.dot(share * scale[:, None], weight.astype(jnp.float32), precision=lax.Precision.HIGHEST)

    ours, theirs = gather(scaled, coded, prepare, add)
    return jax.nn.relu(weighted(ours) + weighted(theirs)).astype(jnp.bfloat16)


def solution(mesh):
    in_specs = (
        P(("row", "rep"), None),
        P(("row", "rep")),
        P("row", "rep", None, None, None, None),
        P("row", "rep", None, None),
        P("row", "rep", None, None),
        P("row", "rep", None),
        P(),
    )
    out_specs = P(("row", "rep"), None)
    return jax.shard_map(local, mesh=mesh, in_specs=in_specs, out_specs=out_specs, check_vma=False)
```

```python
import functools

import jax
import jax.numpy as jnp
import numpy as np
from jax import lax
from jax.experimental import pallas as pl
from jax.experimental.pallas import tpu as pltpu
from jax.sharding import PartitionSpec as P

AXES = ("row", "rep")
TILE = 128
SLOTS = 22
STEPS = 16
N_TILES = STEPS * SLOTS
LIST = 128
BATCH = 4
AT_ONCE = 3
PHASES = 5

HOME = (0, 1, 2, -1)
PIECE = (1, 2, 0, 3)


def member(h, y, z, q):
    return (((h % 2) * 4 + y % 4) * 8 + z % 8) * 4 + q % 4


def up(h, y, z, q):
    return member(h + (q == 3), y, z + 1, q + 1)


def down(h, y, z, q):
    return member(h - (q == 0), y, z - 1, q - 1)


MOVES = {
    "home": (lambda h, y, z, q: member(h, y, z - HOME[q], PIECE[q]), lambda t, h, p, e: (t, h, p, e)),
    "far": (lambda h, y, z, q: member(h + 1, y, z - HOME[q], PIECE[q]), lambda t, h, p, e: (t, 1 - h, p, e)),
    "z1": (lambda *d: down(*d) if d[3] % 2 else up(*d), lambda t, h, p, e: (t, h, (1 - p) % 8, e)),
    "z2": (lambda *d: up(*d) if d[3] % 2 else down(*d), lambda t, h, p, e: (t, h, (-1 - p) % 8, e)),
    "y1": (lambda h, y, z, q: member(h, y ^ (3 if q % 2 else 1), z, q), lambda t, h, p, e: (t, h, p, e ^ 1)),
    "y2": (lambda h, y, z, q: member(h, y ^ (1 if q % 2 else 3), z, q), lambda t, h, p, e: (t, h, p, e ^ 2)),
}


class Blocks:
    def __init__(self, rows, labels):
        self.rows, self.labels = rows, labels

    def __getitem__(self, blocks):
        first, last = blocks.start or 0, len(self.labels) if blocks.stop is None else blocks.stop
        return Blocks(lax.slice_in_dim(self.rows, first * TILE, last * TILE), self.labels[first:last])

    def moved(self, kind):
        sender, relabel = MOVES[kind]
        here = [(h, y, z, q) for h in range(2) for y in range(4) for z in range(8) for q in range(4)]
        rows = lax.ppermute(self.rows, AXES, [(sender(*d), member(*d)) for d in here])
        return Blocks(rows, [relabel(*label) for label in self.labels])

    def half(self, t):
        runs, first = [], 0
        for last in range(1, len(self.labels) + 1):
            if last == len(self.labels) or self.labels[last][0] != self.labels[first][0]:
                if self.labels[first][0] == t:
                    runs.append(self[first:last])
                first = last
        return joined(*runs)


def joined(*parts):
    return Blocks(jnp.concatenate([p.rows for p in parts], 0), [label for p in parts for label in p.labels])


def in_order(parts, *earlier):
    rows = lax.optimization_barrier(tuple(p.rows for p in parts) + earlier)
    return [Blocks(r, p.labels) for r, p in zip(rows, parts)]


def gather(scaled, first_ready, prepare, add):
    own = Blocks(scaled, [(0, 0, 0, 0), (1, 0, 0, 0)])
    near, far = own.moved("home"), own.moved("far")
    (s0,) = in_order([joined(near[0:1], far[0:1], near[1:2], far[1:2])], first_ready)
    s1, e1 = in_order([s0.moved("z1"), s0.moved("y1")])
    ready = prepare(s1.rows)
    s2, e2 = in_order([joined(s0, s1).moved("z2"), joined(s0, e1).moved("y2")], ready)
    b0 = joined(e1.half(1), e2.half(1))
    y12 = joined(s1.half(0), s2.half(0))
    z3, y3 = joined(s2, b0).moved("z1"), y12.moved("y1")
    total = add(None, [s0, s1, e1, s2, e2])
    s3 = z3[0:8].half(0)
    z, y = in_order([joined(z3[0:8], b0, z3[8:14]), joined(y12, y3, s3)], total)
    z4, y4 = z.moved("z2"), y.moved("y2")
    total = add(total, [z3, y3])
    s4 = z4[0:8].half(0)
    z, y = in_order([z4[8:20], joined(s3, y4[12:16], s4)], total)
    z5, y5 = z.moved("z1"), y.moved("y1")
    total = add(total, [z4])
    z, y = in_order([z5, joined(s4, y5[8:12])], total)
    z6, y6 = z.moved("z2"), y.moved("y2")
    total = add(total, [y4, z5, y5])
    return add(total, [z6, y6])


def phase_labels():
    found = []

    def traced(rows):
        return gather(rows, rows, lambda _: rows, lambda _, parts: found.append([label for p in parts for label in p.labels]) or rows)

    jax.eval_shape(traced, jax.ShapeDtypeStruct((2 * TILE, 256), jnp.bfloat16))
    return found


def list_kernel(live, coded, tiles, lists, counts, held, sem):
    load = pltpu.make_async_copy(tiles, held, sem)
    load.start()
    for b in range(8 * PHASES):
        counts[b] = 0

    def one_source(k, _):
        used = live[k]
        for s in range(SLOTS):

            @pl.when(s < used)
            def _(s=s):
                v = coded[k, s]
                b = v >> 17
                n = counts[b]
                lists[b, n] = v & 0x1FFFF
                counts[b] = n + 1

        return 0

    lax.fori_loop(0, STEPS, one_source, 0)
    for b in range(8 * PHASES):
        for i in range(BATCH - 1):
            lists[b, counts[b] + i] = 0
    for i in range(BATCH):
        lists[8 * PHASES, i] = 0
    load.wait()


def slot_lists(live, coded, tiles):
    smem, vmem = pl.BlockSpec(memory_space=pltpu.SMEM), pl.BlockSpec(memory_space=pltpu.VMEM)
    return pl.pallas_call(
        list_kernel,
        out_shape=(
            jax.ShapeDtypeStruct((8 * PHASES + 1, LIST), jnp.int32),
            jax.ShapeDtypeStruct((8 * PHASES,), jnp.int32),
            jax.ShapeDtypeStruct(tiles.shape, tiles.dtype),
        ),
        in_specs=[smem, smem, pl.BlockSpec(memory_space=pltpu.HBM)],
        out_specs=(smem, smem, vmem),
        scratch_shapes=[pltpu.SemaphoreType.DMA],
        compiler_params=pltpu.CompilerParams(vmem_limit_bytes=42 << 20),
        cost_estimate=pl.CostEstimate(flops=0, bytes_accessed=23_000_000, transcendentals=0),
    )(live, coded, tiles)


def product_kernel(buckets, first_bucket, more, lists, counts, tiles, blocks, *refs):
    before, total, order = refs if more else (None, *refs)
    total[...] = before[...] if more else jnp.zeros_like(total)
    end = 0
    for b in range(buckets):

        def note(i, end, b=b):
            order[end] = (b << 16) + ((first_bucket + b) << 8) + i
            return end + 1

        end = lax.fori_loop(0, (counts[first_bucket + b] + (BATCH - 1)) // BATCH, note, end)
    for i in range(AT_ONCE - 1):
        order[end + i] = (8 * PHASES) << 8

    def batches(g, _):
        found = []
        for i in range(AT_ONCE):
            v = order[g * AT_ONCE + i]
            at = [lists[(v >> 8) & 255, (v & 255) * BATCH + j] for j in range(BATCH)]
            left = jnp.concatenate([tiles[a & 1023] for a in at], axis=1)
            right = jnp.concatenate([blocks[a >> 10] for a in at], axis=0)
            found.append((v >> 16, jnp.dot(left, right, preferred_element_type=jnp.float32)))
        for b, product in found:
            total[b >> 1, pl.ds((b & 1) * TILE, TILE), :] += product
        return 0

    lax.fori_loop(0, (end + (AT_ONCE - 1)) // AT_ONCE, batches, 0)


def products(lists, counts, first_bucket, buckets, tiles, blocks, before=None):
    smem, vmem = pl.BlockSpec(memory_space=pltpu.SMEM), pl.BlockSpec(memory_space=pltpu.VMEM)
    more = before is not None
    slots = blocks.shape[0] * 3 * buckets // (8 if buckets < 8 else 32)
    return pl.pallas_call(
        functools.partial(product_kernel, buckets, first_bucket, more),
        out_shape=jax.ShapeDtypeStruct((buckets // 2, 256, 256), jnp.float32),
        in_specs=[smem] * 2 + [vmem] * (2 + more),
        out_specs=vmem,
        scratch_shapes=[pltpu.SMEM((N_TILES // BATCH + 8 + AT_ONCE,), jnp.int32)],
        compiler_params=pltpu.CompilerParams(vmem_limit_bytes=2 << 20),
        cost_estimate=pl.CostEstimate(flops=slots * 8_400_000, bytes_accessed=slots * 150_000, transcendentals=0),
    )(lists, counts, tiles, blocks, *([before] if more else []))


def local(features, degree, tiles, tile_rows, tile_cols, live, weight):
    row, mine = lax.axis_index("row"), lax.axis_index("rep")
    scale = lax.rsqrt(lax.optimization_barrier(degree).astype(jnp.float32))
    first_scale = lax.rsqrt(degree.astype(jnp.float32))
    scaled = (features.astype(jnp.float32) * first_scale[:, None]).astype(jnp.bfloat16)

    cols, steps = tile_cols[0, 0], jnp.arange(STEPS, dtype=jnp.int32)[:, None]
    source = (row - mine - 4 * steps) & 63
    piece, t = cols >> 1, cols & 1
    home = sum(jnp.where(piece == PIECE[i], i, 0) for i in range(4))
    p = ((source & 7) + jnp.where(home == 3, -1, home) - row) & 7
    h = ((source >> 5) - (row >> 5) - ((mine + p) >> 2)) & 1
    core = mine & 1
    p = jnp.where(core == 1, -p & 7, p)
    y = ((source >> 3) ^ (row >> 3)) & 3
    swapped = jnp.where(t == 0, core, home & 1)
    e = jnp.where(y == 2, 3, jnp.where(y == 0, 0, jnp.where(y == 1, 1 + swapped, 2 - swapped)))
    dest = tile_rows[0, 0]
    bucket = ((((dest >> 1) ^ mine) ^ 2) << 1) + (dest & 1)
    label = (((t * 2 + h) * 8 + p) * 4 + e)[..., None]
    places = np.zeros(128, np.int32)
    for n, found in enumerate(phase_labels()):
        for i, (t, h, p, e) in enumerate(found):
            places[((t * 2 + h) * 8 + p) * 4 + e] = ((8 * n) << 17) + ((i + 1) << 10)
    place = jnp.sum(jnp.where(label == jnp.arange(128, dtype=jnp.int32), jnp.asarray(places), 0), axis=-1)
    coded = place + (bucket << 17) + steps * SLOTS + jnp.arange(SLOTS, dtype=jnp.int32)
    lists, counts, held = None, None, None
    devices = range(256)
    nothing = jnp.zeros((TILE, 256), jnp.bfloat16)
    n = 0

    def prepare(earlier):
        nonlocal lists, counts, held
        now, _ = lax.optimization_barrier((coded, earlier))
        lists, counts, held = slot_lists(live[0, 0], now, tiles.reshape(N_TILES, TILE, TILE))
        return counts

    def add(total, found):
        nonlocal n
        first, n = 8 * n, n + 1
        blocks = jnp.concatenate([nothing] + [f.rows for f in found], 0).reshape(-1, TILE, 256)
        if n < PHASES:
            return products(lists, counts, first, 8, held, blocks, total)
        theirs = to_owner_core(products(lists, counts, first, 4, held, blocks, total[0:2]))
        theirs, total = lax.optimization_barrier((theirs, total))
        theirs = lax.ppermute(theirs, AXES, [(i, i ^ 2) for i in devices])
        return to_owner_core(products(lists, counts, first + 4, 4, held, blocks, total[2:4]), 2), theirs

    def to_owner_core(part, pieces=1):
        size = part.shape[1] // pieces
        sent = [part[1, i * size : (i + 1) * size] for i in range(pieces)]
        got = [lax.ppermute(x, AXES, [(i, i ^ 1) for i in devices]) for x in sent]
        return part[0] + jnp.concatenate(got, 0)

    def weighted(share):
        return jnp.dot(share * scale[:, None], weight.astype(jnp.float32), precision=lax.Precision.HIGHEST)

    ours, theirs = gather(scaled, coded, prepare, add)
    return jax.nn.relu(weighted(ours) + weighted(theirs)).astype(jnp.bfloat16)


def solution(mesh):
    in_specs = (
        P(("row", "rep"), None),
        P(("row", "rep")),
        P("row", "rep", None, None, None, None),
        P("row", "rep", None, None),
        P("row", "rep", None, None),
        P("row", "rep", None),
        P(),
    )
    out_specs = P(("row", "rep"), None)
    return jax.shard_map(local, mesh=mesh, in_specs=in_specs, out_specs=out_specs, check_vma=False)
```

```python
import functools

import jax
import jax.numpy as jnp
import numpy as np
from jax import lax
from jax.experimental import pallas as pl
from jax.experimental.pallas import tpu as pltpu
from jax.sharding import PartitionSpec as P

AXES = ("row", "rep")
TILE = 128
SLOTS = 22
STEPS = 16
N_TILES = STEPS * SLOTS
LIST = 128
BATCH = 4
AT_ONCE = 3
PHASES = 5

HOME = (0, 1, 2, -1)
PIECE = (0, 2, 1, 3)


def member(h, y, z, q):
    return (((h % 2) * 4 + y % 4) * 8 + z % 8) * 4 + q % 4


def up(h, y, z, q):
    return member(h + (q == 3), y, z + 1, q + 1)


def down(h, y, z, q):
    return member(h - (q == 0), y, z - 1, q - 1)


MOVES = {
    "home": (lambda h, y, z, q: member(h, y, z - HOME[q], PIECE[q]), lambda t, h, p, e: (t, h, p, e)),
    "far": (lambda h, y, z, q: member(h + 1, y, z - HOME[q], PIECE[q]), lambda t, h, p, e: (t, 1 - h, p, e)),
    "z1": (lambda *d: down(*d) if d[3] % 2 else up(*d), lambda t, h, p, e: (t, h, (1 - p) % 8, e)),
    "z2": (lambda *d: up(*d) if d[3] % 2 else down(*d), lambda t, h, p, e: (t, h, (-1 - p) % 8, e)),
    "y1": (lambda h, y, z, q: member(h, y ^ (3 if q % 2 else 1), z, q), lambda t, h, p, e: (t, h, p, e ^ 1)),
    "y2": (lambda h, y, z, q: member(h, y ^ (1 if q % 2 else 3), z, q), lambda t, h, p, e: (t, h, p, e ^ 2)),
}


class Blocks:
    def __init__(self, rows, labels):
        self.rows, self.labels = rows, labels

    def __getitem__(self, blocks):
        first, last = blocks.start or 0, len(self.labels) if blocks.stop is None else blocks.stop
        return Blocks(lax.slice_in_dim(self.rows, first * TILE, last * TILE), self.labels[first:last])

    def moved(self, kind):
        sender, relabel = MOVES[kind]
        here = [(h, y, z, q) for h in range(2) for y in range(4) for z in range(8) for q in range(4)]
        rows = lax.ppermute(self.rows, AXES, [(sender(*d), member(*d)) for d in here])
        return Blocks(rows, [relabel(*label) for label in self.labels])

    def half(self, t):
        runs, first = [], 0
        for last in range(1, len(self.labels) + 1):
            if last == len(self.labels) or self.labels[last][0] != self.labels[first][0]:
                if self.labels[first][0] == t:
                    runs.append(self[first:last])
                first = last
        return joined(*runs)


def joined(*parts):
    return Blocks(jnp.concatenate([p.rows for p in parts], 0), [label for p in parts for label in p.labels])


def in_order(parts, *earlier):
    rows = lax.optimization_barrier(tuple(p.rows for p in parts) + earlier)
    return [Blocks(r, p.labels) for r, p in zip(rows, parts)]


def gather(scaled, first_ready, prepare, add):
    own = Blocks(scaled, [(0, 0, 0, 0), (1, 0, 0, 0)])
    near, far = own.moved("home"), own.moved("far")
    (s0,) = in_order([joined(near[0:1], far[0:1], near[1:2], far[1:2])], first_ready)
    s1, e1 = in_order([s0.moved("z1"), s0.moved("y1")])
    ready = prepare(s1.rows)
    s2, e2 = in_order([joined(s0, s1).moved("z2"), joined(s0, e1).moved("y2")], ready)
    b0 = joined(e1.half(1), e2.half(1))
    y12 = joined(s1.half(0), s2.half(0))
    z3, y3 = joined(s2, b0).moved("z1"), y12.moved("y1")
    total = add(None, [s0, s1, e1, s2, e2])
    s3 = z3[0:8].half(0)
    z, y = in_order([joined(z3[0:8], b0, z3[8:14]), joined(y12, y3, s3)], total)
    z4, y4 = z.moved("z2"), y.moved("y2")
    total = add(total, [z3, y3])
    s4 = z4[0:8].half(0)
    z, y = in_order([z4[8:20], joined(s3, y4[12:16], s4)], total)
    z5, y5 = z.moved("z1"), y.moved("y1")
    total = add(total, [z4])
    z, y = in_order([z5, joined(s4, y5[8:12])], total)
    z6, y6 = z.moved("z2"), y.moved("y2")
    total = add(total, [y4, z5, y5])
    return add(total, [z6, y6])


def phase_labels():
    found = []

    def traced(rows):
        return gather(rows, rows, lambda _: rows, lambda _, parts: found.append([label for p in parts for label in p.labels]) or rows)

    jax.eval_shape(traced, jax.ShapeDtypeStruct((2 * TILE, 256), jnp.bfloat16))
    return found


def list_kernel(live, coded, tiles, lists, counts, held, sem):
    load = pltpu.make_async_copy(tiles, held, sem)
    load.start()
    for b in range(8 * PHASES):
        counts[b] = 0

    def one_source(k, _):
        used = live[k]
        for s in range(SLOTS):

            @pl.when(s < used)
            def _(s=s):
                v = coded[k, s]
                b = v >> 17
                n = counts[b]
                lists[b, n] = v & 0x1FFFF
                counts[b] = n + 1

        return 0

    lax.fori_loop(0, STEPS, one_source, 0)
    for b in range(8 * PHASES):
        for i in range(BATCH - 1):
            lists[b, counts[b] + i] = 0
    for i in range(BATCH):
        lists[8 * PHASES, i] = 0
    load.wait()


def slot_lists(live, coded, tiles):
    smem, vmem = pl.BlockSpec(memory_space=pltpu.SMEM), pl.BlockSpec(memory_space=pltpu.VMEM)
    return pl.pallas_call(
        list_kernel,
        out_shape=(
            jax.ShapeDtypeStruct((8 * PHASES + 1, LIST), jnp.int32),
            jax.ShapeDtypeStruct((8 * PHASES,), jnp.int32),
            jax.ShapeDtypeStruct(tiles.shape, tiles.dtype),
        ),
        in_specs=[smem, smem, pl.BlockSpec(memory_space=pltpu.HBM)],
        out_specs=(smem, smem, vmem),
        scratch_shapes=[pltpu.SemaphoreType.DMA],
        compiler_params=pltpu.CompilerParams(vmem_limit_bytes=42 << 20),
        cost_estimate=pl.CostEstimate(flops=0, bytes_accessed=23_000_000, transcendentals=0),
    )(live, coded, tiles)


def product_kernel(buckets, first_bucket, more, lists, counts, tiles, blocks, *refs):
    before, total, order = refs if more else (None, *refs)
    total[...] = before[...] if more else jnp.zeros_like(total)
    end = 0
    for b in range(buckets):

        def note(i, end, b=b):
            order[end] = (b << 16) + ((first_bucket + b) << 8) + i
            return end + 1

        end = lax.fori_loop(0, (counts[first_bucket + b] + (BATCH - 1)) // BATCH, note, end)
    for i in range(AT_ONCE - 1):
        order[end + i] = (8 * PHASES) << 8

    def batches(g, _):
        found = []
        for i in range(AT_ONCE):
            v = order[g * AT_ONCE + i]
            at = [lists[(v >> 8) & 255, (v & 255) * BATCH + j] for j in range(BATCH)]
            left = jnp.concatenate([tiles[a & 1023] for a in at], axis=1)
            right = jnp.concatenate([blocks[a >> 10] for a in at], axis=0)
            found.append((v >> 16, jnp.dot(left, right, preferred_element_type=jnp.float32)))
        for b, product in found:
            total[b >> 1, pl.ds((b & 1) * TILE, TILE), :] += product
        return 0

    lax.fori_loop(0, (end + (AT_ONCE - 1)) // AT_ONCE, batches, 0)


def products(lists, counts, first_bucket, buckets, tiles, blocks, before=None):
    smem, vmem = pl.BlockSpec(memory_space=pltpu.SMEM), pl.BlockSpec(memory_space=pltpu.VMEM)
    more = before is not None
    slots = blocks.shape[0] * 3 * buckets // (8 if buckets < 8 else 32)
    return pl.pallas_call(
        functools.partial(product_kernel, buckets, first_bucket, more),
        out_shape=jax.ShapeDtypeStruct((buckets // 2, 256, 256), jnp.float32),
        in_specs=[smem] * 2 + [vmem] * (2 + more),
        out_specs=vmem,
        scratch_shapes=[pltpu.SMEM((N_TILES // BATCH + 8 + AT_ONCE,), jnp.int32)],
        compiler_params=pltpu.CompilerParams(vmem_limit_bytes=2 << 20),
        cost_estimate=pl.CostEstimate(flops=slots * 8_400_000, bytes_accessed=slots * 150_000, transcendentals=0),
    )(lists, counts, tiles, blocks, *([before] if more else []))


def local(features, degree, tiles, tile_rows, tile_cols, live, weight):
    row, mine = lax.axis_index("row"), lax.axis_index("rep")
    scale = lax.rsqrt(lax.optimization_barrier(degree).astype(jnp.float32))
    first_scale = lax.rsqrt(degree.astype(jnp.float32))
    scaled = (features.astype(jnp.float32) * first_scale[:, None]).astype(jnp.bfloat16)

    cols, steps = tile_cols[0, 0], jnp.arange(STEPS, dtype=jnp.int32)[:, None]
    source = (row - mine - 4 * steps) & 63
    piece, t = cols >> 1, cols & 1
    home = sum(jnp.where(piece == PIECE[i], i, 0) for i in range(4))
    p = ((source & 7) + jnp.where(home == 3, -1, home) - row) & 7
    h = ((source >> 5) - (row >> 5) - ((mine + p) >> 2)) & 1
    core = mine & 1
    p = jnp.where(core == 1, -p & 7, p)
    y = ((source >> 3) ^ (row >> 3)) & 3
    swapped = jnp.where(t == 0, core, home & 1)
    e = jnp.where(y == 2, 3, jnp.where(y == 0, 0, jnp.where(y == 1, 1 + swapped, 2 - swapped)))
    dest = tile_rows[0, 0]
    bucket = ((((dest >> 1) ^ mine) ^ 2) << 1) + (dest & 1)
    label = (((t * 2 + h) * 8 + p) * 4 + e)[..., None]
    places = np.zeros(128, np.int32)
    for n, found in enumerate(phase_labels()):
        for i, (t, h, p, e) in enumerate(found):
            places[((t * 2 + h) * 8 + p) * 4 + e] = ((8 * n) << 17) + ((i + 1) << 10)
    place = jnp.sum(jnp.where(label == jnp.arange(128, dtype=jnp.int32), jnp.asarray(places), 0), axis=-1)
    coded = place + (bucket << 17) + steps * SLOTS + jnp.arange(SLOTS, dtype=jnp.int32)
    lists, counts, held = None, None, None
    devices = range(256)
    nothing = jnp.zeros((TILE, 256), jnp.bfloat16)
    n = 0

    def prepare(earlier):
        nonlocal lists, counts, held
        now, _ = lax.optimization_barrier((coded, earlier))
        lists, counts, held = slot_lists(live[0, 0], now, tiles.reshape(N_TILES, TILE, TILE))
        return counts

    def add(total, found):
        nonlocal n
        first, n = 8 * n, n + 1
        blocks = jnp.concatenate([nothing] + [f.rows for f in found], 0).reshape(-1, TILE, 256)
        if n < PHASES:
            return products(lists, counts, first, 8, held, blocks, total)
        theirs = to_owner_core(products(lists, counts, first, 4, held, blocks, total[0:2]))
        theirs, total = lax.optimization_barrier((theirs, total))
        theirs = lax.ppermute(theirs, AXES, [(i, i ^ 2) for i in devices])
        return to_owner_core(products(lists, counts, first + 4, 4, held, blocks, total[2:4]), 2), theirs

    def to_owner_core(part, pieces=1):
        size = part.shape[1] // pieces
        sent = [part[1, i * size : (i + 1) * size] for i in range(pieces)]
        got = [lax.ppermute(x, AXES, [(i, i ^ 1) for i in devices]) for x in sent]
        return part[0] + jnp.concatenate(got, 0)

    def weighted(share):
        return jnp.dot(share * scale[:, None], weight.astype(jnp.float32), precision=lax.Precision.HIGHEST)

    ours, theirs = gather(scaled, coded, prepare, add)
    return jax.nn.relu(weighted(ours) + weighted(theirs)).astype(jnp.bfloat16)


def solution(mesh):
    in_specs = (
        P(("row", "rep"), None),
        P(("row", "rep")),
        P("row", "rep", None, None, None, None),
        P("row", "rep", None, None),
        P("row", "rep", None, None),
        P("row", "rep", None),
        P(),
    )
    out_specs = P(("row", "rep"), None)
    return jax.shard_map(local, mesh=mesh, in_specs=in_specs, out_specs=out_specs, check_vma=False)
```

```python
import functools

import jax
import jax.numpy as jnp
import numpy as np
from jax import lax
from jax.experimental import pallas as pl
from jax.experimental.pallas import tpu as pltpu
from jax.sharding import PartitionSpec as P

AXES = ("row", "rep")
TILE = 128
SLOTS = 22
STEPS = 16
N_TILES = STEPS * SLOTS
LIST = 128
BATCH = 4
AT_ONCE = 4
PHASES = 5

HOME = (0, 1, 2, -1)
PIECE = (0, 2, 1, 3)


def member(h, y, z, q):
    return (((h % 2) * 4 + y % 4) * 8 + z % 8) * 4 + q % 4


def up(h, y, z, q):
    return member(h + (q == 3), y, z + 1, q + 1)


def down(h, y, z, q):
    return member(h - (q == 0), y, z - 1, q - 1)


MOVES = {
    "home": (lambda h, y, z, q: member(h, y, z - HOME[q], PIECE[q]), lambda t, h, p, e: (t, h, p, e)),
    "far": (lambda h, y, z, q: member(h + 1, y, z - HOME[q], PIECE[q]), lambda t, h, p, e: (t, 1 - h, p, e)),
    "z1": (lambda *d: down(*d) if d[3] % 2 else up(*d), lambda t, h, p, e: (t, h, (1 - p) % 8, e)),
    "z2": (lambda *d: up(*d) if d[3] % 2 else down(*d), lambda t, h, p, e: (t, h, (-1 - p) % 8, e)),
    "y1": (lambda h, y, z, q: member(h, y ^ (3 if q % 2 else 1), z, q), lambda t, h, p, e: (t, h, p, e ^ 1)),
    "y2": (lambda h, y, z, q: member(h, y ^ (1 if q % 2 else 3), z, q), lambda t, h, p, e: (t, h, p, e ^ 2)),
}


class Blocks:
    def __init__(self, rows, labels):
        self.rows, self.labels = rows, labels

    def __getitem__(self, blocks):
        first, last = blocks.start or 0, len(self.labels) if blocks.stop is None else blocks.stop
        return Blocks(lax.slice_in_dim(self.rows, first * TILE, last * TILE), self.labels[first:last])

    def moved(self, kind):
        sender, relabel = MOVES[kind]
        here = [(h, y, z, q) for h in range(2) for y in range(4) for z in range(8) for q in range(4)]
        rows = lax.ppermute(self.rows, AXES, [(sender(*d), member(*d)) for d in here])
        return Blocks(rows, [relabel(*label) for label in self.labels])

    def half(self, t):
        runs, first = [], 0
        for last in range(1, len(self.labels) + 1):
            if last == len(self.labels) or self.labels[last][0] != self.labels[first][0]:
                if self.labels[first][0] == t:
                    runs.append(self[first:last])
                first = last
        return joined(*runs)


def joined(*parts):
    return Blocks(jnp.concatenate([p.rows for p in parts], 0), [label for p in parts for label in p.labels])


def in_order(parts, *earlier):
    rows = lax.optimization_barrier(tuple(p.rows for p in parts) + earlier)
    return [Blocks(r, p.labels) for r, p in zip(rows, parts)]


def gather(scaled, first_ready, prepare, add):
    own = Blocks(scaled, [(0, 0, 0, 0), (1, 0, 0, 0)])
    near, far = own.moved("home"), own.moved("far")
    (s0,) = in_order([joined(near[0:1], far[0:1], near[1:2], far[1:2])], first_ready)
    s1, e1 = in_order([s0.moved("z1"), s0.moved("y1")])
    ready = prepare(s1.rows)
    s2, e2 = in_order([joined(s0, s1).moved("z2"), joined(s0, e1).moved("y2")], ready)
    b0 = joined(e1.half(1), e2.half(1))
    y12 = joined(s1.half(0), s2.half(0))
    z3, y3 = joined(s2, b0).moved("z1"), y12.moved("y1")
    total = add(None, [s0, s1, e1, s2, e2])
    s3 = z3[0:8].half(0)
    z, y = in_order([joined(z3[0:8], b0, z3[8:14]), joined(y12, y3, s3)], total)
    z4, y4 = z.moved("z2"), y.moved("y2")
    total = add(total, [z3, y3])
    s4 = z4[0:8].half(0)
    z, y = in_order([z4[8:20], joined(s3, y4[12:16], s4)], total)
    z5, y5 = z.moved("z1"), y.moved("y1")
    total = add(total, [z4])
    z, y = in_order([z5, joined(s4, y5[8:12])], total)
    z6, y6 = z.moved("z2"), y.moved("y2")
    total = add(total, [y4, z5, y5])
    return add(total, [z6, y6])


def phase_labels():
    found = []

    def traced(rows):
        return gather(rows, rows, lambda _: rows, lambda _, parts: found.append([label for p in parts for label in p.labels]) or rows)

    jax.eval_shape(traced, jax.ShapeDtypeStruct((2 * TILE, 256), jnp.bfloat16))
    return found


def list_kernel(live, coded, tiles, lists, counts, held, sem):
    load = pltpu.make_async_copy(tiles, held, sem)
    load.start()
    for b in range(8 * PHASES):
        counts[b] = 0

    def one_source(k, _):
        used = live[k]
        for s in range(SLOTS):

            @pl.when(s < used)
            def _(s=s):
                v = coded[k, s]
                b = v >> 17
                n = counts[b]
                lists[b, n] = v & 0x1FFFF
                counts[b] = n + 1

        return 0

    lax.fori_loop(0, STEPS, one_source, 0)
    for b in range(8 * PHASES):
        for i in range(BATCH - 1):
            lists[b, counts[b] + i] = 0
    for i in range(BATCH):
        lists[8 * PHASES, i] = 0
    load.wait()


def slot_lists(live, coded, tiles):
    smem, vmem = pl.BlockSpec(memory_space=pltpu.SMEM), pl.BlockSpec(memory_space=pltpu.VMEM)
    return pl.pallas_call(
        list_kernel,
        out_shape=(
            jax.ShapeDtypeStruct((8 * PHASES + 1, LIST), jnp.int32),
            jax.ShapeDtypeStruct((8 * PHASES,), jnp.int32),
            jax.ShapeDtypeStruct(tiles.shape, tiles.dtype),
        ),
        in_specs=[smem, smem, pl.BlockSpec(memory_space=pltpu.HBM)],
        out_specs=(smem, smem, vmem),
        scratch_shapes=[pltpu.SemaphoreType.DMA],
        compiler_params=pltpu.CompilerParams(vmem_limit_bytes=42 << 20),
        cost_estimate=pl.CostEstimate(flops=0, bytes_accessed=23_000_000, transcendentals=0),
    )(live, coded, tiles)


def product_kernel(buckets, first_bucket, more, lists, counts, tiles, blocks, *refs):
    before, total, order = refs if more else (None, *refs)
    total[...] = before[...] if more else jnp.zeros_like(total)
    end = 0
    for b in range(buckets):

        def note(i, end, b=b):
            order[end] = (b << 16) + ((first_bucket + b) << 8) + i
            return end + 1

        end = lax.fori_loop(0, (counts[first_bucket + b] + (BATCH - 1)) // BATCH, note, end)
    for i in range(AT_ONCE - 1):
        order[end + i] = (8 * PHASES) << 8

    def batches(g, _):
        found = []
        for i in range(AT_ONCE):
            v = order[g * AT_ONCE + i]
            at = [lists[(v >> 8) & 255, (v & 255) * BATCH + j] for j in range(BATCH)]
            left = jnp.concatenate([tiles[a & 1023] for a in at], axis=1)
            right = jnp.concatenate([blocks[a >> 10] for a in at], axis=0)
            found.append((v >> 16, jnp.dot(left, right, preferred_element_type=jnp.float32)))
        for b, product in found:
            total[b >> 1, pl.ds((b & 1) * TILE, TILE), :] += product
        return 0

    lax.fori_loop(0, (end + (AT_ONCE - 1)) // AT_ONCE, batches, 0)


def products(lists, counts, first_bucket, buckets, tiles, blocks, before=None):
    smem, vmem = pl.BlockSpec(memory_space=pltpu.SMEM), pl.BlockSpec(memory_space=pltpu.VMEM)
    more = before is not None
    slots = blocks.shape[0] * 3 * buckets // (8 if buckets < 8 else 32)
    return pl.pallas_call(
        functools.partial(product_kernel, buckets, first_bucket, more),
        out_shape=jax.ShapeDtypeStruct((buckets // 2, 256, 256), jnp.float32),
        in_specs=[smem] * 2 + [vmem] * (2 + more),
        out_specs=vmem,
        scratch_shapes=[pltpu.SMEM((N_TILES // BATCH + 8 + AT_ONCE,), jnp.int32)],
        compiler_params=pltpu.CompilerParams(vmem_limit_bytes=2 << 20),
        cost_estimate=pl.CostEstimate(flops=slots * 8_400_000, bytes_accessed=slots * 150_000, transcendentals=0),
    )(lists, counts, tiles, blocks, *([before] if more else []))


def local(features, degree, tiles, tile_rows, tile_cols, live, weight):
    row, mine = lax.axis_index("row"), lax.axis_index("rep")
    scale = lax.rsqrt(lax.optimization_barrier(degree).astype(jnp.float32))
    first_scale = lax.rsqrt(degree.astype(jnp.float32))
    scaled = (features.astype(jnp.float32) * first_scale[:, None]).astype(jnp.bfloat16)

    cols, steps = tile_cols[0, 0], jnp.arange(STEPS, dtype=jnp.int32)[:, None]
    source = (row - mine - 4 * steps) & 63
    piece, t = cols >> 1, cols & 1
    home = sum(jnp.where(piece == PIECE[i], i, 0) for i in range(4))
    p = ((source & 7) + jnp.where(home == 3, -1, home) - row) & 7
    h = ((source >> 5) - (row >> 5) - ((mine + p) >> 2)) & 1
    core = mine & 1
    p = jnp.where(core == 1, -p & 7, p)
    y = ((source >> 3) ^ (row >> 3)) & 3
    swapped = jnp.where(t == 0, core, home & 1)
    e = jnp.where(y == 2, 3, jnp.where(y == 0, 0, jnp.where(y == 1, 1 + swapped, 2 - swapped)))
    dest = tile_rows[0, 0]
    bucket = ((((dest >> 1) ^ mine) ^ 2) << 1) + (dest & 1)
    label = (((t * 2 + h) * 8 + p) * 4 + e)[..., None]
    places = np.zeros(128, np.int32)
    for n, found in enumerate(phase_labels()):
        for i, (t, h, p, e) in enumerate(found):
            places[((t * 2 + h) * 8 + p) * 4 + e] = ((8 * n) << 17) + ((i + 1) << 10)
    place = jnp.sum(jnp.where(label == jnp.arange(128, dtype=jnp.int32), jnp.asarray(places), 0), axis=-1)
    coded = place + (bucket << 17) + steps * SLOTS + jnp.arange(SLOTS, dtype=jnp.int32)
    lists, counts, held = None, None, None
    devices = range(256)
    nothing = jnp.zeros((TILE, 256), jnp.bfloat16)
    n = 0

    def prepare(earlier):
        nonlocal lists, counts, held
        now, _ = lax.optimization_barrier((coded, earlier))
        lists, counts, held = slot_lists(live[0, 0], now, tiles.reshape(N_TILES, TILE, TILE))
        return counts

    def add(total, found):
        nonlocal n
        first, n = 8 * n, n + 1
        blocks = jnp.concatenate([nothing] + [f.rows for f in found], 0).reshape(-1, TILE, 256)
        if n < PHASES:
            return products(lists, counts, first, 8, held, blocks, total)
        theirs = to_owner_core(products(lists, counts, first, 4, held, blocks, total[0:2]))
        theirs, total = lax.optimization_barrier((theirs, total))
        theirs = lax.ppermute(theirs, AXES, [(i, i ^ 2) for i in devices])
        return to_owner_core(products(lists, counts, first + 4, 4, held, blocks, total[2:4]), 2), theirs

    def to_owner_core(part, pieces=1):
        size = part.shape[1] // pieces
        sent = [part[1, i * size : (i + 1) * size] for i in range(pieces)]
        got = [lax.ppermute(x, AXES, [(i, i ^ 1) for i in devices]) for x in sent]
        return part[0] + jnp.concatenate(got, 0)

    def weighted(share):
        return jnp.dot(share * scale[:, None], weight.astype(jnp.float32), precision=lax.Precision.HIGHEST)

    ours, theirs = gather(scaled, coded, prepare, add)
    return jax.nn.relu(weighted(ours) + weighted(theirs)).astype(jnp.bfloat16)


def solution(mesh):
    in_specs = (
        P(("row", "rep"), None),
        P(("row", "rep")),
        P("row", "rep", None, None, None, None),
        P("row", "rep", None, None),
        P("row", "rep", None, None),
        P("row", "rep", None),
        P(),
    )
    out_specs = P(("row", "rep"), None)
    return jax.shard_map(local, mesh=mesh, in_specs=in_specs, out_specs=out_specs, check_vma=False)
```
